32 devices in a mesh: groups: 2 (over x), outer: 2 (over core), inner: 8 (over z, y).
Axes of the slice: x: 2, y: 2, z: 4, core: 2. Of those that a mesh axis runs over, the one named last changes fastest.
Arguments:
- hidden_states: bfloat16 [768, 3584], P(('groups', 'outer', 'inner')), parts along dimension 0, may hold values from -6 to 6
- expert_ids: int32 [768, 8], P(('groups', 'outer', 'inner')), parts along dimension 0, may hold values from 0 to 31, all different within a row; in each aligned block of 24 rows (0 to 23, 24 to 47, ...) at most 12 rows name the same one
- gate_scores: float32 [768, 8], P(('groups', 'outer', 'inner')), parts along dimension 0, may hold values from -6 to 6
- w_gate: bfloat16 [32, 3584, 1024], P('inner', None, 'outer'), may hold values from -0.09375 to 0.09375
- w_up: bfloat16 [32, 3584, 1024], P('inner', None, 'outer'), may hold values from -0.09375 to 0.09375
- w_down: bfloat16 [32, 1024, 3584], P('inner', 'outer'), may hold values from -0.1875 to 0.1875
Outputs:
- moe_out: bfloat16 [768, 3584], P(('groups', 'outer', 'inner')), parts along dimension 0
The draws below stay inside these ranges and needn't reach their ends.
There are 2 independent parts, one for each index of `groups`. The reference program is written for one: setup_inputs(seed, part) draws one part's arguments, and reference() takes and returns one part's arrays. A program takes and returns all parts, laid end to end along the dimension named above; an argument that names none is the same for every part. Nothing has to cross between parts.
Inputs may be any that keep to these rules, and one draw needn't show every extreme that they name: `expert_ids`: each row names 8 different experts; in each aligned block of 24 rows (the tokens of one device) no expert is named by more than 12 rows, a bound that some block reaches.
All inputs are finite; a program needn't handle non-finite values.
Results may differ from the reference program's by a relative error of at most 0.012.
Values may be sent and summed in bfloat16 or wider, within the bound.
No kernel may reach another device: no remote copies, remote signals or barrier semaphores. Data moves between devices by JAX's collectives and lax.ppermute only.
A program may use at most 128 MiB of HBM per device.

```python
import math
import jax
import jax.numpy as jnp
import numpy as np
from jax import lax

D = 3584
FF = 1024
TOP = 8
EXPERTS = 32
TOK_DEV = 24
MOST = 12
TOKENS = 384
N_OUTER = 2


def level_of(own_key, extent, cuts, least, largest):
    level, own = 1.0, jax.random.fold_in(own_key, 6)
    for axis_at, blocks in cuts:
        steps = jnp.exp(jax.random.uniform(jax.random.fold_in(own, axis_at), (blocks,), jnp.float32, least / len(cuts), largest / len(cuts)))
        level = level * jnp.repeat(steps, extent[axis_at] // blocks).reshape([-1 if axis == axis_at else 1 for axis in range(len(extent))])
    return level


def routed_block(own_key, own, number, rows, number_of, top, limit, lean):
    order = jax.random.permutation(own_key, number_of)
    crowded, usual = portions_of(number_of, rows * top, limit, lean, True), portions_of(number_of, rows * top, limit, lean, False)
    places = jnp.arange(number_of)

    def named(lengths, offset_by):
        used = int((lengths > 0).sum())
        fixed = max(1, used // 4)
        moved = fixed + (places - fixed + offset_by * (used - fixed)) % max(1, number_of - fixed)
        return jnp.zeros((number_of,), jnp.int32).at[order[jnp.where(places < fixed, places, moved)]].set(jnp.asarray(lengths, jnp.int32))

    lengths = jnp.where(number % 4 == 0, named(crowded, number // 4), named(usual, number - number // 4 - 1))
    mixed = jax.random.permutation(jax.random.fold_in(own, 3), number_of)
    source_of, taker = mixed[0:number_of // 2 * 2:2], mixed[1:number_of // 2 * 2:2]
    slack = jnp.minimum(lengths[source_of] - 1, limit - lengths[taker]) // 2
    slack = jnp.where((source_of == order[0]) | (taker == order[0]) | (lengths[taker] == 0), 0, jnp.maximum(slack, 0))
    moved = jax.random.randint(jax.random.fold_in(own, 4), (number_of // 2,), 0, 1 << 20) % (slack + 1)
    lengths = lengths.at[source_of].add(-moved).at[taker].add(moved)
    members = jnp.searchsorted(jnp.cumsum(lengths), jnp.arange(rows * top), side="right").astype(jnp.int32)
    listing = members.reshape(top, rows).T
    listing = listing[jax.random.permutation(jax.random.fold_in(own, 1), rows)]
    offset_by = jax.random.randint(jax.random.fold_in(own, 2), (rows, 1), 0, top)
    return jnp.take_along_axis(listing, (jnp.arange(top)[None, :] + offset_by) % top, axis=1)


def portions_of(amount, total, bound, skew, full):
    weights = [(1 << 20) // math.isqrt(grade ** skew) + 1 for grade in range(1, amount + 1)]
    largest = bound if full else min(bound, max(-(-total // amount), total * weights[0] // sum(weights)))
    least = 1 if total - largest >= amount - 1 else 0
    given, surplus = [largest] + [least] * (amount - 1), total - largest - least * (amount - 1)
    while surplus > 0:
        movable = [i for i in range(1, amount) if given[i] < largest] or [i for i in range(1, amount) if given[i] < bound]
        pool, remaining = sum([weights[i] for i in movable]), surplus
        for i in movable:
            addition = min(bound - given[i], max(1, remaining * weights[i] // pool), surplus)
            given[i] = given[i] + addition
            surplus = surplus - addition
    return np.array(given)


def centred(rng, extent, width, bound, cuts=(), kind=jnp.bfloat16):
    array = width * jax.random.normal(rng, extent, jnp.float32)
    if cuts:
        array = array * level_of(rng, extent, cuts, -0.22, 0.18)
    return jnp.clip(array, -bound, bound).astype(kind)


def setup_inputs(seed: int = 0, part: int = 0) -> dict:
    seeds = jax.random.split(jax.random.key(seed), 7)
    part_keys = jax.random.split(jax.random.fold_in(seeds[6], part), 7)
    hidden_states = centred(part_keys[0], (TOKENS, D), 1.0, 6.0, ((0, 16),))
    expert_ids_keys = jax.random.split(jax.random.fold_in(part_keys[1], 1), TOKENS // TOK_DEV)
    expert_ids_turns = jax.random.permutation(jax.random.fold_in(part_keys[1], 3), TOKENS // TOK_DEV)
    expert_ids = jax.vmap(lambda own, number: routed_block(jax.random.fold_in(part_keys[1], 2), own, number, TOK_DEV, EXPERTS, TOP, MOST, 2))(expert_ids_keys, expert_ids_turns).reshape((TOKENS, TOP))
    gate_scores = centred(part_keys[2], (TOKENS, TOP), 1.5, 6.0, ((0, 16),), jnp.float32)
    w_gate = centred(seeds[3], (EXPERTS, D, FF), D ** -0.5, 0.09375, ((0, 8), (2, 2)))
    w_up = centred(seeds[4], (EXPERTS, D, FF), D ** -0.5, 0.09375, ((0, 8), (2, 2)))
    w_down = centred(seeds[5], (EXPERTS, FF, D), FF ** -0.5, 0.1875, ((0, 8), (1, 2)))
    return {"hidden_states": hidden_states, "expert_ids": expert_ids, "gate_scores": gate_scores, "w_gate": w_gate, "w_up": w_up, "w_down": w_down}


def reference(hidden_states, expert_ids, gate_scores, w_gate, w_up, w_down):
    devices = TOKENS // TOK_DEV
    ids_block = expert_ids.reshape(devices, TOK_DEV * TOP).astype(jnp.int32)
    onehot = (ids_block[..., None] == jnp.arange(EXPERTS, dtype=jnp.int32)).astype(jnp.int32)
    ranking = jnp.sum((jnp.cumsum(onehot, axis=1).astype(jnp.int32) - onehot) * onehot, axis=2).astype(jnp.int32)
    device_of = jnp.broadcast_to(jnp.arange(devices, dtype=jnp.int32)[:, None], ids_block.shape)
    pair_of = jnp.broadcast_to(jnp.arange(TOK_DEV * TOP, dtype=jnp.int32)[None, :], ids_block.shape)
    token_of = (device_of * TOK_DEV + pair_of // TOP).astype(jnp.int32)
    row_table = jnp.full((EXPERTS, devices, MOST), TOKENS, jnp.int32)
    row_table = row_table.at[ids_block, device_of, ranking].set(token_of)
    padded = jnp.concatenate([hidden_states, jnp.zeros((1, D), hidden_states.dtype)], axis=0)

    def per_expert(operands):
        rows_index, gate_w, up_w, down_w = operands
        rows = padded[rows_index.reshape(-1)]
        gate = jnp.dot(rows, gate_w, preferred_element_type=jnp.float32)
        upper = jnp.dot(rows, up_w, preferred_element_type=jnp.float32)
        hidden = (jax.nn.silu(gate) * upper).astype(jnp.bfloat16)
        blocks = hidden.reshape(rows.shape[0], N_OUTER, FF // N_OUTER).astype(jnp.float32)
        down_blocks = down_w.reshape(N_OUTER, FF // N_OUTER, D).astype(jnp.float32)
        partial_value = jnp.einsum("nhf,hfd->hnd", blocks, down_blocks).astype(jnp.bfloat16)
        return jnp.sum(partial_value.astype(jnp.float32), axis=0).astype(jnp.bfloat16)

    outputs_all = lax.map(per_expert, (row_table, w_gate, w_up, w_down))
    picked = outputs_all[ids_block, device_of * MOST + ranking]
    picked = picked.reshape(TOKENS, TOP, D).astype(jnp.float32)
    sigmoid_vals = jax.nn.sigmoid(gate_scores.astype(jnp.float32))
    weights = 2.5 * sigmoid_vals / jnp.sum(sigmoid_vals, axis=1, keepdims=True)
    return jnp.sum(weights[..., None] * picked, axis=1).astype(jnp.bfloat16)
```

```python
import functools

import jax
import jax.numpy as jnp
from jax import lax
from jax.experimental import pallas as pl
from jax.experimental.pallas import tpu as pltpu
from jax.sharding import PartitionSpec as P

LANES = 128
SPLIT = 2
VMEM_LIMIT = 60 * 1024 * 1024


def routing_columns(expert_ids, gate_scores, experts):
    sigmoid_vals = jax.nn.sigmoid(gate_scores)
    weights = 2.5 * sigmoid_vals / jnp.sum(sigmoid_vals, axis=1, keepdims=True)
    named = expert_ids[..., None] == jnp.arange(experts, dtype=jnp.int32)
    dense = jnp.sum(jnp.where(named, weights[..., None], 0.0), axis=1)
    high = lax.reduce_precision(dense, 8, 7)
    both = jnp.concatenate([high, dense - high], axis=1).astype(jnp.bfloat16)
    return jnp.pad(both, ((0, 0), (0, LANES - 2 * experts)))


def up_kernel(experts, local_experts, index_ref, rows_ref, gate_w_ref, up_w_ref, out_ref):
    model_width = gate_w_ref.shape[1]
    x = rows_ref[:, :model_width]
    gate = jnp.dot(x, gate_w_ref[0], preferred_element_type=jnp.float32)
    upper = jnp.dot(x, up_w_ref[0], preferred_element_type=jnp.float32)
    expert = index_ref[0] * local_experts + pl.program_id(0)
    columns = rows_ref[:, model_width:].astype(jnp.float32)
    lane = lax.broadcasted_iota(jnp.int32, columns.shape, 1)
    mine = (lane == expert) | (lane == expert + experts)
    weight = jnp.sum(jnp.where(mine, columns, 0.0), axis=1, keepdims=True)
    hidden = gate / (1.0 + jnp.exp(-gate)) * upper * weight
    out_ref[...] = hidden.astype(jnp.bfloat16)


def down_kernel(hidden_ref, down_w_ref, out_ref):
    block = down_w_ref[...]
    block = block.reshape(block.shape[0] * block.shape[1], block.shape[2])
    out_ref[...] = jnp.dot(
        hidden_ref[...], block, preferred_element_type=jnp.float32
    ).astype(jnp.bfloat16)


def expert_rows(rows, w_gate, w_up, w_down, inner_index, experts):
    local_experts, model_width, width = w_gate.shape
    count = rows.shape[0]
    part = width // SPLIT
    hidden = pl.pallas_call(
        functools.partial(up_kernel, experts, local_experts),
        grid=(local_experts, SPLIT),
        in_specs=[
            pl.BlockSpec(memory_space=pltpu.SMEM),
            pl.BlockSpec((count, rows.shape[1]), lambda l, s: (0, 0)),
            pl.BlockSpec((1, model_width, part), lambda l, s: (l, 0, s)),
            pl.BlockSpec((1, model_width, part), lambda l, s: (l, 0, s)),
        ],
        out_specs=pl.BlockSpec((count, part), lambda l, s: (0, l * SPLIT + s)),
        out_shape=jax.ShapeDtypeStruct((count, local_experts * width), jnp.bfloat16),
        compiler_params=pltpu.CompilerParams(vmem_limit_bytes=VMEM_LIMIT),
        name="gate_up",
    )(inner_index, rows, w_gate, w_up)
    tile = 512
    return pl.pallas_call(
        down_kernel,
        grid=(model_width // tile,),
        in_specs=[
            pl.BlockSpec(hidden.shape, lambda n: (0, 0)),
            pl.BlockSpec((local_experts, width, tile), lambda n: (0, 0, n)),
        ],
        out_specs=pl.BlockSpec((count, tile), lambda n: (0, n)),
        out_shape=jax.ShapeDtypeStruct((count, model_width), jnp.bfloat16),
        compiler_params=pltpu.CompilerParams(vmem_limit_bytes=VMEM_LIMIT),
        name="down",
    )(hidden, w_down)


def swap_core(value):
    return lax.ppermute(value, "outer", [(0, 1), (1, 0)])


def swap_inner(value, bit):
    return lax.ppermute(value, "inner", [(i, i ^ bit) for i in range(8)])


def add(a, b):
    return (a.astype(jnp.float32) + b.astype(jnp.float32)).astype(jnp.bfloat16)


def on_device(hidden_states, expert_ids, gate_scores, w_gate, w_up, w_down):
    local_experts = w_gate.shape[0]
    inner_size = lax.axis_size("inner")
    experts = local_experts * inner_size
    count = hidden_states.shape[0]
    inner_index = lax.axis_index("inner").astype(jnp.int32).reshape(1)
    own = jnp.concatenate(
        [hidden_states, routing_columns(expert_ids, gate_scores, experts)], axis=1
    )
    compute = functools.partial(
        expert_rows, w_gate=w_gate, w_up=w_up, w_down=w_down, inner_index=inner_index,
        experts=experts,
    )
    if inner_size != 8 or lax.axis_size("outer") != 2:
        everyone = lax.all_gather(own, ("outer", "inner"), axis=0, tiled=True)
        return lax.psum_scatter(
            compute(everyone), ("outer", "inner"), scatter_dimension=0, tiled=True
        )

    column = [own] + [swap_inner(own, bit) for bit in (2, 4, 6)]
    partner = [swap_inner(block, 1) for block in column]
    near, far = jnp.concatenate(column), jnp.concatenate(partner)
    everyone = jnp.concatenate([near, swap_core(near), far, swap_core(far)])
    outs = compute(everyone)
    group = 4 * count
    near_sum, near_other, far_sum, far_other = (
        outs[i * group : (i + 1) * group] for i in range(4)
    )
    far_sum = add(far_sum, swap_core(far_other))
    near_sum = add(near_sum, swap_core(near_other))
    total = None
    for step in (3, 2, 1, 0):
        part = slice(step * count, (step + 1) * count)
        arrived = swap_inner(far_sum[part], 1)
        if step:
            term = swap_inner(add(near_sum[part], arrived), 2 * step).astype(jnp.float32)
        else:
            term = near_sum[part].astype(jnp.float32) + arrived.astype(jnp.float32)
        total = term if total is None else total + term
    return total.astype(jnp.bfloat16)


def solution(mesh):
    return jax.shard_map(
        on_device,
        mesh=mesh,
        in_specs=(
            P(("groups", "outer", "inner"), None),
            P(("groups", "outer", "inner"), None),
            P(("groups", "outer", "inner"), None),
            P("inner", None, "outer"),
            P("inner", None, "outer"),
            P("inner", "outer", None),
        ),
        out_specs=P(("groups", "outer", "inner"), None),
        check_vma=False,
    )
```

```python
import functools

import jax
import jax.numpy as jnp
from jax import lax
from jax.experimental import pallas as pl
from jax.experimental.pallas import tpu as pltpu
from jax.sharding import PartitionSpec as P

LANES = 128
MIB = 1024 * 1024
TILE = 512
VMEM = pl.BlockSpec(memory_space=pltpu.VMEM)
HBM = pl.BlockSpec(memory_space=pltpu.HBM)
SMEM = pl.BlockSpec(memory_space=pltpu.SMEM)


def send_kernel(experts, rows_ref, ids_ref, scores_ref, out_ref):
    sigmoid_vals = jax.nn.sigmoid(scores_ref[...])
    weights = 2.5 * sigmoid_vals / jnp.sum(sigmoid_vals, axis=0, keepdims=True)
    top, count = weights.shape
    expert = lax.broadcasted_iota(jnp.int32, (experts, count), 0)
    dense = jnp.zeros((experts, count), jnp.float32)
    for k in range(top):
        dense += jnp.where(expert == ids_ref[k : k + 1, :], weights[k : k + 1, :], 0.0)
    high = lax.reduce_precision(dense, 8, 7)
    rest = jnp.zeros((LANES - 2 * experts, count), jnp.float32)
    table = jnp.concatenate([high, dense - high, rest]).astype(jnp.bfloat16)
    same = lax.broadcasted_iota(jnp.int32, (count, count), 0)
    same = same == lax.broadcasted_iota(jnp.int32, (count, count), 1)
    columns = lax.dot_general(
        same.astype(jnp.float32).astype(jnp.bfloat16),
        table,
        (((1,), (1,)), ((), ())),
        preferred_element_type=jnp.float32,
    )
    width = rows_ref.shape[1]
    out_ref[:, :width] = rows_ref[...]
    out_ref[:, width:] = columns.astype(jnp.bfloat16)


def with_routing(rows, expert_ids, gate_scores, experts):
    count, width = rows.shape
    return pl.pallas_call(
        functools.partial(send_kernel, experts),
        in_specs=[VMEM] * 3,
        out_specs=VMEM,
        out_shape=jax.ShapeDtypeStruct((count, width + LANES), jnp.bfloat16),
        compiler_params=pltpu.CompilerParams(vmem_limit_bytes=4 * MIB),
        name="with_routing",
    )(rows, expert_ids.T, gate_scores.T)


def weight_of(columns, expert, experts):
    lane = lax.broadcasted_iota(jnp.int32, columns.shape, 1)
    mine = (lane == expert) | (lane == expert + experts)
    return jnp.sum(jnp.where(mine, columns, 0.0), axis=1, keepdims=True)


def hidden_of(x, gate_w, up_w, weight):
    gate = jnp.dot(x, gate_w, preferred_element_type=jnp.float32)
    upper = jnp.dot(x, up_w, preferred_element_type=jnp.float32)
    return (gate / (1.0 + jnp.exp(-gate)) * upper * weight).astype(jnp.bfloat16)


def stream_up_kernel(experts, local_experts, index_ref, rows_ref, gate_w_ref, up_w_ref, out_ref):
    model_width = gate_w_ref.shape[1]
    expert = index_ref[0] * local_experts + pl.program_id(0)
    weight = weight_of(rows_ref[:, model_width:].astype(jnp.float32), expert, experts)
    out_ref[...] = hidden_of(rows_ref[:, :model_width], gate_w_ref[0], up_w_ref[0], weight)


def stream_down_kernel(hidden_ref, down_w_ref, out_ref):
    block = down_w_ref[...]
    block = block.reshape(block.shape[0] * block.shape[1], block.shape[2])
    out_ref[...] = jnp.dot(
        hidden_ref[...], block, preferred_element_type=jnp.float32
    ).astype(jnp.bfloat16)


def stream_rows(rows, w_gate, w_up, w_down, inner_index, experts):
    local_experts, model_width, width = w_gate.shape
    count, part = rows.shape[0], width // 2
    hidden = pl.pallas_call(
        functools.partial(stream_up_kernel, experts, local_experts),
        grid=(local_experts, 2),
        in_specs=[
            pl.BlockSpec(memory_space=pltpu.SMEM),
            pl.BlockSpec((count, rows.shape[1]), lambda l, s: (0, 0)),
            pl.BlockSpec((1, model_width, part), lambda l, s: (l, 0, s)),
            pl.BlockSpec((1, model_width, part), lambda l, s: (l, 0, s)),
        ],
        out_specs=pl.BlockSpec((count, part), lambda l, s: (0, l * 2 + s)),
        out_shape=jax.ShapeDtypeStruct((count, local_experts * width), jnp.bfloat16),
        compiler_params=pltpu.CompilerParams(vmem_limit_bytes=60 * MIB),
        name="stream_gate_up",
    )(inner_index, rows, w_gate, w_up)
    return pl.pallas_call(
        stream_down_kernel,
        grid=(model_width // TILE,),
        in_specs=[
            pl.BlockSpec(hidden.shape, lambda n: (0, 0)),
            pl.BlockSpec((local_experts, width, TILE), lambda n: (0, 0, n)),
        ],
        out_specs=pl.BlockSpec((count, TILE), lambda n: (0, n)),
        out_shape=jax.ShapeDtypeStruct((count, model_width), jnp.bfloat16),
        compiler_params=pltpu.CompilerParams(vmem_limit_bytes=60 * MIB),
        name="stream_down",
    )(hidden, w_down)


def load_kernel(source_ref, copy_ref, sem):
    copy = pltpu.make_async_copy(source_ref, copy_ref, sem)
    copy.start()
    copy.wait()


def load(weights):
    size = weights.size * weights.dtype.itemsize
    return pl.pallas_call(
        load_kernel,
        in_specs=[pl.BlockSpec(memory_space=pltpu.HBM)],
        out_specs=VMEM,
        out_shape=pltpu.VMEM(weights.shape, weights.dtype),
        scratch_shapes=[pltpu.SemaphoreType.DMA],
        compiler_params=pltpu.CompilerParams(vmem_limit_bytes=MIB),
        cost_estimate=pl.CostEstimate(flops=0, bytes_accessed=2 * size, transcendentals=0),
        name="load",
    )(weights)


def assemble(row_refs, x_ref):
    rows = jnp.concatenate([ref[...].astype(jnp.float32) for ref in row_refs])
    width = x_ref.shape[1]
    x_ref[...] = rows[:, :width].astype(jnp.bfloat16)
    return rows[:, width:]


def near_kernel(experts, blocks, index_ref, *refs):
    rows, (gate_w, up_source, out, up_w, x, gates, sems) = refs[:blocks], refs[blocks:]
    local_experts, _, width = gate_w.shape
    copies = [
        pltpu.make_async_copy(up_source.at[l], up_w.at[l], sems.at[l])
        for l in range(local_experts)
    ]
    for copy in copies:
        copy.start()
    columns = assemble(rows, x)
    for l in range(local_experts):
        part = slice(l * width, (l + 1) * width)
        gates[:, part] = jnp.dot(x[...], gate_w[l], preferred_element_type=jnp.float32)
    for l in range(local_experts):
        part = slice(l * width, (l + 1) * width)
        weight = weight_of(columns, index_ref[0] * local_experts + l, experts)
        copies[l].wait()
        gate = gates[:, part]
        upper = jnp.dot(x[...], up_w[l], preferred_element_type=jnp.float32)
        out[:, part] = (gate / (1.0 + jnp.exp(-gate)) * upper * weight).astype(jnp.bfloat16)


def near_rows(blocks, w_gate, w_up, inner_index, experts):
    local_experts, model_width, width = w_gate.shape
    count = sum(block.shape[0] for block in blocks)
    return pl.pallas_call(
        functools.partial(near_kernel, experts, len(blocks)),
        in_specs=[SMEM] + [VMEM] * (len(blocks) + 1) + [HBM],
        out_specs=[VMEM] * 2,
        out_shape=[
            jax.ShapeDtypeStruct((count, local_experts * width), jnp.bfloat16),
            pltpu.VMEM(w_up.shape, w_up.dtype),
        ],
        scratch_shapes=[
            pltpu.VMEM((count, model_width), jnp.bfloat16),
            pltpu.VMEM((count, local_experts * width), jnp.float32),
            pltpu.SemaphoreType.DMA((local_experts,)),
        ],
        compiler_params=pltpu.CompilerParams(vmem_limit_bytes=8 * MIB),
        cost_estimate=pl.CostEstimate(
            flops=4 * count * model_width * width * local_experts,
            bytes_accessed=0,
            transcendentals=0,
        ),
        name="near_rows",
    )(inner_index, *blocks, w_gate, w_up)


def fetch(source_ref, first, block_ref, sems):
    copies = []
    for at in range(0, block_ref.shape[2], TILE):
        size = min(TILE, block_ref.shape[2] - at)
        copy = pltpu.make_async_copy(
            source_ref.at[:, :, pl.ds(first + at, size)],
            block_ref.at[:, :, pl.ds(at, size)],
            sems.at[at // TILE],
        )
        copy.start()
        copies.append((at, size, copy))
    return copies


def down_into(copies, hidden_ref, block_ref, near_out, far_out, other_out):
    half = near_out.shape[0]
    for at, size, copy in copies:
        copy.wait()
        block = block_ref[:, :, at : at + size].reshape(-1, size)
        value = jnp.dot(hidden_ref[...], block, preferred_element_type=jnp.float32)
        value = value.astype(jnp.bfloat16)
        near_out[:, at : at + size] = value[:half]
        other_out[:half, at : at + size] = value[half : 2 * half]
        far_out[:, at : at + size] = value[2 * half : 3 * half]
        other_out[half:, at : at + size] = value[3 * half :]


def far_kernel(experts, blocks, index_ref, *refs):
    rows, rest = refs[:blocks], refs[blocks:]
    gate_w, up_w, near, down_w, hidden, near_out, far_out, other_out, x, block, sems = rest
    local_experts, _, width = gate_w.shape
    copies = fetch(down_w, 0, block, sems)
    columns = assemble(rows, x)
    count = near.shape[0]
    hidden[:count] = near[...]
    for l in range(local_experts):
        weight = weight_of(columns, index_ref[0] * local_experts + l, experts)
        hidden[count:, l * width : (l + 1) * width] = hidden_of(
            x[...], gate_w[l], up_w[l], weight
        )
    down_into(copies, hidden, block, near_out, far_out, other_out)


def down_kernel(first, hidden, down_w, near_out, far_out, other_out, block, sems):
    down_into(
        fetch(down_w, first, block, sems), hidden, block, near_out, far_out, other_out
    )


def sums(half, columns):
    return [
        jax.ShapeDtypeStruct((rows, columns), jnp.bfloat16) for rows in (half, half, 2 * half)
    ]


def tiles(local_experts, width, columns):
    return [
        pltpu.VMEM((local_experts, width, columns), jnp.bfloat16),
        pltpu.SemaphoreType.DMA((pl.cdiv(columns, TILE),)),
    ]


def far_rows(blocks, w_gate, w_up, near, w_down, inner_index, experts, cut):
    count, depth = near.shape
    local_experts, width, model_width = w_down.shape
    return pl.pallas_call(
        functools.partial(far_kernel, experts, len(blocks)),
        in_specs=[SMEM] + [VMEM] * (len(blocks) + 3) + [HBM],
        out_specs=[VMEM] * 4,
        out_shape=[jax.ShapeDtypeStruct((2 * count, depth), near.dtype)]
        + sums(count // 2, cut),
        scratch_shapes=[pltpu.VMEM((count, model_width), jnp.bfloat16)]
        + tiles(local_experts, width, cut),
        compiler_params=pltpu.CompilerParams(vmem_limit_bytes=15 * MIB),
        name="far_rows",
    )(inner_index, *blocks, w_gate, w_up, near, w_down)


def down(hidden, w_down, first):
    local_experts, width, model_width = w_down.shape
    columns = model_width - first
    return pl.pallas_call(
        functools.partial(down_kernel, first),
        in_specs=[VMEM, HBM],
        out_specs=[VMEM] * 3,
        out_shape=sums(hidden.shape[0] // 4, columns),
        scratch_shapes=tiles(local_experts, width, columns),
        compiler_params=pltpu.CompilerParams(vmem_limit_bytes=15 * MIB),
        cost_estimate=pl.CostEstimate(
            flops=2 * hidden.size * columns, bytes_accessed=0, transcendentals=0
        ),
        name="down",
    )(hidden, w_down)


def swap_core(value):
    return lax.ppermute(value, "outer", [(0, 1), (1, 0)])


def swap_inner(value, bit):
    return lax.ppermute(value, "inner", [(i, i ^ bit) for i in range(8)])


def tie(*values):
    return lax.optimization_barrier(values)


def wide(value):
    return value.astype(jnp.float32)


def on_device(hidden_states, expert_ids, gate_scores, w_gate, w_up, w_down):
    local_experts, model_width, _ = w_gate.shape
    inner_size = lax.axis_size("inner")
    experts = local_experts * inner_size
    count = hidden_states.shape[0]
    inner_index = lax.axis_index("inner").astype(jnp.int32).reshape(1)
    own = with_routing(hidden_states, expert_ids, gate_scores, experts)
    if inner_size != 8 or lax.axis_size("outer") != 2:
        everyone = lax.all_gather(own, ("outer", "inner"), axis=0, tiled=True)
        outs = stream_rows(everyone, w_gate, w_up, w_down, inner_index, experts)
        return lax.psum_scatter(outs, ("outer", "inner"), scatter_dimension=0, tiled=True)

    w_gate, w_up, w_down = (
        pltpu.with_memory_space_constraint(w, pltpu.HBM) for w in (w_gate, w_up, w_down)
    )
    own, inner_index = tie(own, inner_index)
    z1, y0, z2 = swap_inner(own, 2), swap_inner(own, 1), swap_inner(own, 4)
    w_gate = load(w_gate)
    own, z1, z2, y0, w_gate = tie(own, z1, z2, y0, w_gate)
    z3, y1, y2 = swap_inner(own, 6), swap_inner(z1, 1), swap_inner(z2, 1)
    y3 = swap_inner(z3, 1)
    near = [own, z1, z2, z3]
    near += [swap_core(block) for block in near]
    hidden, w_up = near_rows(near, w_gate, w_up, inner_index, experts)
    hidden, y3 = tie(hidden, y3)
    far = [y0, y1, y2, y3]
    far += [swap_core(block) for block in far]

    cut = (model_width // LANES * 5 // 7) * LANES
    group = 4 * count

    def rows(step):
        return slice(step * count, (step + 1) * count)

    hidden, near_a, far_a, other_a = far_rows(
        far, w_gate, w_up, hidden, w_down, inner_index, experts, cut
    )
    other_a = swap_core(other_a)
    far_a = (wide(far_a) + wide(other_a[group:])).astype(jnp.bfloat16)
    far_a, hidden = tie(far_a, hidden)
    across = swap_inner(far_a, 1)
    near_b, far_b, other_b = down(hidden, w_down, cut)
    other_b = swap_core(other_b)

    both = jnp.stack([near_b, far_b]).reshape(2, 4, count, -1)
    both = wide(both) + wide(other_b.reshape(2, 4, count, -1))
    sent_b = [swap_inner(both[:, step].astype(jnp.bfloat16), 2 * step) for step in (3, 2, 1)]
    across, *sent_b = tie(across, *sent_b)

    total_a = wide(near_a) + wide(other_a[:group]) + wide(across)
    sent_a = [
        swap_inner(total_a[rows(step)].astype(jnp.bfloat16), 2 * step) for step in (3, 2, 1)
    ]
    sum_b = sum((wide(block) for block in sent_b), both[:, 0])
    sum_b = sum_b[0] + wide(swap_inner(sum_b[1].astype(jnp.bfloat16), 1))
    sum_a = sum((wide(block) for block in sent_a), total_a[rows(0)])
    return jnp.concatenate([sum_a, sum_b], axis=1).astype(jnp.bfloat16)


def solution(mesh):
    return jax.shard_map(
        on_device,
        mesh=mesh,
        in_specs=(
            P(("groups", "outer", "inner"), None),
            P(("groups", "outer", "inner"), None),
            P(("groups", "outer", "inner"), None),
            P("inner", None, "outer"),
            P("inner", None, "outer"),
            P("inner", "outer", None),
        ),
        out_specs=P(("groups", "outer", "inner"), None),
        check_vma=False,
    )
```

```python
import functools

import jax
import jax.numpy as jnp
from jax import lax
from jax.experimental import pallas as pl
from jax.experimental.pallas import tpu as pltpu
from jax.sharding import PartitionSpec as P

LANES = 128
MIB = 1024 * 1024
TILE = 512
SLOTS = 4
VMEM = pl.BlockSpec(memory_space=pltpu.VMEM)
HBM = pl.BlockSpec(memory_space=pltpu.HBM)
SMEM = pl.BlockSpec(memory_space=pltpu.SMEM)


def send_kernel(experts, rows_hbm, ids_hbm, scores_hbm, out_ref, rows, ids, scores, sems):
    pairs = ((rows_hbm, rows), (ids_hbm, ids), (scores_hbm, scores))
    copies = [pltpu.make_async_copy(*pair, sems.at[i]) for i, pair in enumerate(pairs)]
    for copy in copies:
        copy.start()
    copies[1].wait()
    copies[2].wait()
    sigmoid_vals = jax.nn.sigmoid(scores[...])
    weights = 2.5 * sigmoid_vals / jnp.sum(sigmoid_vals, axis=0, keepdims=True)
    top, count = weights.shape
    expert = lax.broadcasted_iota(jnp.int32, (experts, count), 0)
    dense = jnp.zeros((experts, count), jnp.float32)
    for k in range(top):
        dense += jnp.where(expert == ids[k : k + 1, :], weights[k : k + 1, :], 0.0)
    high = lax.reduce_precision(dense, 8, 7)
    rest = jnp.zeros((LANES - 2 * experts, count), jnp.float32)
    table = jnp.concatenate([high, dense - high, rest]).astype(jnp.bfloat16)
    same = lax.broadcasted_iota(jnp.int32, (count, count), 0)
    same = same == lax.broadcasted_iota(jnp.int32, (count, count), 1)
    columns = lax.dot_general(
        same.astype(jnp.float32).astype(jnp.bfloat16),
        table,
        (((1,), (1,)), ((), ())),
        preferred_element_type=jnp.float32,
    )
    width = rows.shape[1]
    out_ref[:, width:] = columns.astype(jnp.bfloat16)
    copies[0].wait()
    out_ref[:, :width] = rows[...]


def with_routing(rows, expert_ids, gate_scores, experts):
    count, width = rows.shape
    arrays = [
        pltpu.with_memory_space_constraint(array, pltpu.HBM)
        for array in (rows, expert_ids.T, gate_scores.T)
    ]
    return pl.pallas_call(
        functools.partial(send_kernel, experts),
        in_specs=[HBM] * 3,
        out_specs=VMEM,
        out_shape=jax.ShapeDtypeStruct((count, width + LANES), jnp.bfloat16),
        scratch_shapes=[pltpu.VMEM(array.shape, array.dtype) for array in arrays]
        + [pltpu.SemaphoreType.DMA((3,))],
        compiler_params=pltpu.CompilerParams(vmem_limit_bytes=4 * MIB),
        name="with_routing",
    )(*arrays)


def weight_of(columns, expert, experts):
    lane = lax.broadcasted_iota(jnp.int32, columns.shape, 1)
    mine = (lane == expert) | (lane == expert + experts)
    return jnp.sum(jnp.where(mine, columns, 0.0), axis=1, keepdims=True)


def hidden_of(x, gate_w, up_w, weight):
    gate = jnp.dot(x, gate_w, preferred_element_type=jnp.float32)
    upper = jnp.dot(x, up_w, preferred_element_type=jnp.float32)
    return (gate / (1.0 + jnp.exp(-gate)) * upper * weight).astype(jnp.bfloat16)


def stream_up_kernel(experts, local_experts, index_ref, rows_ref, gate_w_ref, up_w_ref, out_ref):
    model_width = gate_w_ref.shape[1]
    expert = index_ref[0] * local_experts + pl.program_id(0)
    weight = weight_of(rows_ref[:, model_width:].astype(jnp.float32), expert, experts)
    out_ref[...] = hidden_of(rows_ref[:, :model_width], gate_w_ref[0], up_w_ref[0], weight)


def stream_down_kernel(hidden_ref, down_w_ref, out_ref):
    block = down_w_ref[...]
    block = block.reshape(block.shape[0] * block.shape[1], block.shape[2])
    out_ref[...] = jnp.dot(
        hidden_ref[...], block, preferred_element_type=jnp.float32
    ).astype(jnp.bfloat16)


def stream_rows(rows, w_gate, w_up, w_down, inner_index, experts):
    local_experts, model_width, width = w_gate.shape
    count, part = rows.shape[0], width // 2
    hidden = pl.pallas_call(
        functools.partial(stream_up_kernel, experts, local_experts),
        grid=(local_experts, 2),
        in_specs=[
            pl.BlockSpec(memory_space=pltpu.SMEM),
            pl.BlockSpec((count, rows.shape[1]), lambda l, s: (0, 0)),
            pl.BlockSpec((1, model_width, part), lambda l, s: (l, 0, s)),
            pl.BlockSpec((1, model_width, part), lambda l, s: (l, 0, s)),
        ],
        out_specs=pl.BlockSpec((count, part), lambda l, s: (0, l * 2 + s)),
        out_shape=jax.ShapeDtypeStruct((count, local_experts * width), jnp.bfloat16),
        compiler_params=pltpu.CompilerParams(vmem_limit_bytes=60 * MIB),
        name="stream_gate_up",
    )(inner_index, rows, w_gate, w_up)
    return pl.pallas_call(
        stream_down_kernel,
        grid=(model_width // TILE,),
        in_specs=[
            pl.BlockSpec(hidden.shape, lambda n: (0, 0)),
            pl.BlockSpec((local_experts, width, TILE), lambda n: (0, 0, n)),
        ],
        out_specs=pl.BlockSpec((count, TILE), lambda n: (0, n)),
        out_shape=jax.ShapeDtypeStruct((count, model_width), jnp.bfloat16),
        compiler_params=pltpu.CompilerParams(vmem_limit_bytes=60 * MIB),
        name="stream_down",
    )(hidden, w_down)


def load_kernel(source_ref, copy_ref, sem):
    copy = pltpu.make_async_copy(source_ref, copy_ref, sem)
    copy.start()
    copy.wait()


def load(weights):
    size = weights.size * weights.dtype.itemsize
    return pl.pallas_call(
        load_kernel,
        in_specs=[pl.BlockSpec(memory_space=pltpu.HBM)],
        out_specs=VMEM,
        out_shape=pltpu.VMEM(weights.shape, weights.dtype),
        scratch_shapes=[pltpu.SemaphoreType.DMA],
        compiler_params=pltpu.CompilerParams(vmem_limit_bytes=MIB),
        cost_estimate=pl.CostEstimate(flops=0, bytes_accessed=2 * size, transcendentals=0),
        name="load",
    )(weights)


def assemble(row_refs, x_ref):
    rows = jnp.concatenate([ref[...].astype(jnp.float32) for ref in row_refs])
    width = x_ref.shape[1]
    x_ref[...] = rows[:, :width].astype(jnp.bfloat16)
    return rows[:, width:]


def near_kernel(experts, blocks, index_ref, *refs):
    rows, (gate_w, up_source, out, up_w, x, gates, sems) = refs[:blocks], refs[blocks:]
    local_experts, _, width = gate_w.shape
    copies = [
        pltpu.make_async_copy(up_source.at[l], up_w.at[l], sems.at[l])
        for l in range(local_experts)
    ]
    for copy in copies:
        copy.start()
    columns = assemble(rows, x)
    ahead = local_experts // 2

    def gate_of(l):
        gates[:, l * width : (l + 1) * width] = jnp.dot(
            x[...], gate_w[l], preferred_element_type=jnp.float32
        )

    for l in range(ahead):
        gate_of(l)
    for l in range(local_experts):
        if l + ahead < local_experts:
            gate_of(l + ahead)
        part = slice(l * width, (l + 1) * width)
        weight = weight_of(columns, index_ref[0] * local_experts + l, experts)
        copies[l].wait()
        gate = gates[:, part]
        upper = jnp.dot(x[...], up_w[l], preferred_element_type=jnp.float32)
        out[:, part] = (gate / (1.0 + jnp.exp(-gate)) * upper * weight).astype(jnp.bfloat16)


def near_rows(blocks, w_gate, w_up, inner_index, experts):
    local_experts, model_width, width = w_gate.shape
    count = sum(block.shape[0] for block in blocks)
    return pl.pallas_call(
        functools.partial(near_kernel, experts, len(blocks)),
        in_specs=[SMEM] + [VMEM] * (len(blocks) + 1) + [HBM],
        out_specs=[VMEM] * 2,
        out_shape=[
            jax.ShapeDtypeStruct((count, local_experts * width), jnp.bfloat16),
            pltpu.VMEM(w_up.shape, w_up.dtype),
        ],
        scratch_shapes=[
            pltpu.VMEM((count, model_width), jnp.bfloat16),
            pltpu.VMEM((count, local_experts * width), jnp.float32),
            pltpu.SemaphoreType.DMA((local_experts,)),
        ],
        compiler_params=pltpu.CompilerParams(vmem_limit_bytes=8 * MIB),
        cost_estimate=pl.CostEstimate(
            flops=4 * count * model_width * width * local_experts,
            bytes_accessed=0,
            transcendentals=0,
        ),
        name="near_rows",
    )(inner_index, *blocks, w_gate, w_up)


def tile_copies(source_ref, slots_ref, sems):
    copies = []
    for at in range(0, source_ref.shape[2], TILE):
        slot = at // TILE % slots_ref.shape[0]
        copy = pltpu.make_async_copy(
            source_ref.at[:, :, pl.ds(at, TILE)], slots_ref.at[slot], sems.at[slot]
        )
        copies.append((at, slot, copy))
    return copies


def far_kernel(experts, blocks, cut, index_ref, *refs):
    rows, rest = refs[:blocks], refs[blocks:]
    gate_w, up_w, near, down_w, own_a, near_a, far_a, own_b, other_b = rest[:9]
    x, hidden, slots, sems = rest[9:]
    local_experts, _, width = gate_w.shape
    copies = tile_copies(down_w, slots, sems)
    for _, _, copy in copies[:SLOTS]:
        copy.start()
    columns = assemble(rows, x)
    count = near.shape[0]
    half = count // 2
    hidden[:count] = near[...]
    for l in range(local_experts):
        weight = weight_of(columns, index_ref[0] * local_experts + l, experts)
        hidden[count:, l * width : (l + 1) * width] = hidden_of(
            x[...], gate_w[l], up_w[l], weight
        )
    for i, (at, slot, copy) in enumerate(copies):
        copy.wait()
        value = jnp.dot(
            hidden[...],
            slots[slot].reshape(-1, TILE),
            preferred_element_type=jnp.float32,
        ).astype(jnp.bfloat16)
        if i + SLOTS < len(copies):
            copies[i + SLOTS][2].start()
        own, start = (own_a, 0) if at < cut else (own_b, cut)
        to = slice(at - start, at - start + TILE)
        own[:half, to] = value[:half]
        own[half:, to] = value[count : count + half]
        if at < cut:
            near_a[:, to] = value[half:count]
            far_a[:, to] = value[count + half :]
        else:
            other_b[:half, to] = value[half:count]
            other_b[half:, to] = value[count + half :]


def far_rows(blocks, w_gate, w_up, near, w_down, inner_index, experts, cut):
    count, depth = near.shape
    local_experts, width, model_width = w_down.shape
    return pl.pallas_call(
        functools.partial(far_kernel, experts, len(blocks), cut),
        in_specs=[SMEM] + [VMEM] * (len(blocks) + 3) + [HBM],
        out_specs=[VMEM] * 5,
        out_shape=[
            jax.ShapeDtypeStruct(shape, jnp.bfloat16)
            for shape in (
                (count, cut),
                (count // 2, cut),
                (count // 2, cut),
                (count, model_width - cut),
                (count, model_width - cut),
            )
        ],
        scratch_shapes=[
            pltpu.VMEM((count, model_width), jnp.bfloat16),
            pltpu.VMEM((2 * count, depth), jnp.bfloat16),
            pltpu.VMEM((SLOTS, local_experts, width, TILE), w_down.dtype),
            pltpu.SemaphoreType.DMA((SLOTS,)),
        ],
        compiler_params=pltpu.CompilerParams(vmem_limit_bytes=14 * MIB),
        name="far_rows",
    )(inner_index, *blocks, w_gate, w_up, near, w_down)


def swap_core(value):
    return lax.ppermute(value, "outer", [(0, 1), (1, 0)])


def swap_inner(value, bit):
    return lax.ppermute(value, "inner", [(i, i ^ bit) for i in range(8)])


def tie(*values):
    return lax.optimization_barrier(values)


def wide(value):
    return value.astype(jnp.float32)


def on_device(hidden_states, expert_ids, gate_scores, w_gate, w_up, w_down):
    local_experts, model_width, _ = w_gate.shape
    inner_size = lax.axis_size("inner")
    experts = local_experts * inner_size
    count = hidden_states.shape[0]
    inner_index = lax.axis_index("inner").astype(jnp.int32).reshape(1)
    own = with_routing(hidden_states, expert_ids, gate_scores, experts)
    if inner_size != 8 or lax.axis_size("outer") != 2:
        everyone = lax.all_gather(own, ("outer", "inner"), axis=0, tiled=True)
        outs = stream_rows(everyone, w_gate, w_up, w_down, inner_index, experts)
        return lax.psum_scatter(outs, ("outer", "inner"), scatter_dimension=0, tiled=True)

    w_gate, w_up, w_down = (
        pltpu.with_memory_space_constraint(w, pltpu.HBM) for w in (w_gate, w_up, w_down)
    )
    own, inner_index = tie(own, inner_index)
    z1, y0, z2 = swap_inner(own, 2), swap_inner(own, 1), swap_inner(own, 4)
    w_gate = load(w_gate)
    own, z1, z2, y0, w_gate = tie(own, z1, z2, y0, w_gate)
    z3, y1, y2 = swap_inner(own, 6), swap_inner(z1, 1), swap_inner(z2, 1)
    y3 = swap_inner(z3, 1)
    near = [own, z1, z2, z3]
    near += [swap_core(block) for block in near]
    hidden, w_up = near_rows(near, w_gate, w_up, inner_index, experts)
    hidden, y2, y3 = tie(hidden, y2, y3)
    far = [y0, y1, y2, y3]
    far += [swap_core(block) for block in far]

    cut = (model_width // LANES * 5 // 7) * LANES
    own_a, near_a, far_a, own_b, other_b = far_rows(
        far, w_gate, w_up, hidden, w_down, inner_index, experts, cut
    )
    group = 4 * count
    far_a = (wide(own_a[group:]) + wide(swap_core(far_a))).astype(jnp.bfloat16)
    near_a = wide(own_a[:group]) + wide(swap_core(near_a))
    across = swap_inner(far_a, 1)
    both = (wide(own_b) + wide(swap_core(other_b))).reshape(2, 4, count, -1)
    sent_b = [swap_inner(both[:, step].astype(jnp.bfloat16), 2 * step) for step in (3, 2, 1)]
    across, *sent_b = tie(across, *sent_b)
    sums_a = near_a + wide(across)
    sent_a = [
        swap_inner(sums_a[at * count : (at + 1) * count].astype(jnp.bfloat16), 2 * at)
        for at in (3, 2, 1)
    ]
    sum_b = sum((wide(block) for block in sent_b), both[:, 0])
    sum_b = sum_b[0] + wide(swap_inner(sum_b[1].astype(jnp.bfloat16), 1))
    sum_a = sum((wide(block) for block in sent_a), sums_a[:count])
    return jnp.concatenate([sum_a, sum_b], axis=1).astype(jnp.bfloat16)


def solution(mesh):
    return jax.shard_map(
        on_device,
        mesh=mesh,
        in_specs=(
            P(("groups", "outer", "inner"), None),
            P(("groups", "outer", "inner"), None),
            P(("groups", "outer", "inner"), None),
            P("inner", None, "outer"),
            P("inner", None, "outer"),
            P("inner", "outer", None),
        ),
        out_specs=P(("groups", "outer", "inner"), None),
        check_vma=False,
    )
```

```python
import functools

import jax
import jax.numpy as jnp
from jax import lax
from jax.experimental import pallas as pl
from jax.experimental.pallas import tpu as pltpu
from jax.sharding import PartitionSpec as P

LANES = 128
MIB = 1024 * 1024
TILE = 512
SLOTS = 4
VMEM = pl.BlockSpec(memory_space=pltpu.VMEM)
HBM = pl.BlockSpec(memory_space=pltpu.HBM)
SMEM = pl.BlockSpec(memory_space=pltpu.SMEM)


def send_kernel(experts, rows_hbm, ids_hbm, scores_hbm, out_ref, rows, ids, scores, sems):
    pairs = ((rows_hbm, rows), (ids_hbm, ids), (scores_hbm, scores))
    copies = [pltpu.make_async_copy(*pair, sems.at[i]) for i, pair in enumerate(pairs)]
    for copy in copies:
        copy.start()
    copies[1].wait()
    copies[2].wait()
    sigmoid_vals = jax.nn.sigmoid(scores[...])
    weights = 2.5 * sigmoid_vals / jnp.sum(sigmoid_vals, axis=0, keepdims=True)
    top, count = weights.shape
    expert = lax.broadcasted_iota(jnp.int32, (experts, count), 0)
    dense = jnp.zeros((experts, count), jnp.float32)
    for k in range(top):
        dense += jnp.where(expert == ids[k : k + 1, :], weights[k : k + 1, :], 0.0)
    high = lax.reduce_precision(dense, 8, 7)
    rest = jnp.zeros((LANES - 2 * experts, count), jnp.float32)
    table = jnp.concatenate([high, dense - high, rest]).astype(jnp.bfloat16)
    same = lax.broadcasted_iota(jnp.int32, (count, count), 0)
    same = same == lax.broadcasted_iota(jnp.int32, (count, count), 1)
    columns = lax.dot_general(
        same.astype(jnp.float32).astype(jnp.bfloat16),
        table,
        (((1,), (1,)), ((), ())),
        preferred_element_type=jnp.float32,
    )
    width = rows.shape[1]
    out_ref[:, width:] = columns.astype(jnp.bfloat16)
    copies[0].wait()
    out_ref[:, :width] = rows[...]


def with_routing(rows, expert_ids, gate_scores, experts):
    count, width = rows.shape
    arrays = [
        pltpu.with_memory_space_constraint(array, pltpu.HBM)
        for array in (rows, expert_ids.T, gate_scores.T)
    ]
    return pl.pallas_call(
        functools.partial(send_kernel, experts),
        in_specs=[HBM] * 3,
        out_specs=VMEM,
        out_shape=jax.ShapeDtypeStruct((count, width + LANES), jnp.bfloat16),
        scratch_shapes=[pltpu.VMEM(array.shape, array.dtype) for array in arrays]
        + [pltpu.SemaphoreType.DMA((3,))],
        compiler_params=pltpu.CompilerParams(vmem_limit_bytes=4 * MIB),
        name="with_routing",
    )(*arrays)


def weight_of(columns, expert, experts):
    lane = lax.broadcasted_iota(jnp.int32, columns.shape, 1)
    mine = (lane == expert) | (lane == expert + experts)
    return jnp.sum(jnp.where(mine, columns, 0.0), axis=1, keepdims=True)


def hidden_of(x, gate_w, up_w, weight):
    gate = jnp.dot(x, gate_w, preferred_element_type=jnp.float32)
    upper = jnp.dot(x, up_w, preferred_element_type=jnp.float32)
    return (gate / (1.0 + jnp.exp(-gate)) * upper * weight).astype(jnp.bfloat16)


def stream_up_kernel(experts, local_experts, index_ref, rows_ref, gate_w_ref, up_w_ref, out_ref):
    model_width = gate_w_ref.shape[1]
    expert = index_ref[0] * local_experts + pl.program_id(0)
    weight = weight_of(rows_ref[:, model_width:].astype(jnp.float32), expert, experts)
    out_ref[...] = hidden_of(rows_ref[:, :model_width], gate_w_ref[0], up_w_ref[0], weight)


def stream_down_kernel(hidden_ref, down_w_ref, out_ref):
    block = down_w_ref[...]
    block = block.reshape(block.shape[0] * block.shape[1], block.shape[2])
    out_ref[...] = jnp.dot(
        hidden_ref[...], block, preferred_element_type=jnp.float32
    ).astype(jnp.bfloat16)


def stream_rows(rows, w_gate, w_up, w_down, inner_index, experts):
    local_experts, model_width, width = w_gate.shape
    count, part = rows.shape[0], width // 2
    hidden = pl.pallas_call(
        functools.partial(stream_up_kernel, experts, local_experts),
        grid=(local_experts, 2),
        in_specs=[
            pl.BlockSpec(memory_space=pltpu.SMEM),
            pl.BlockSpec((count, rows.shape[1]), lambda l, s: (0, 0)),
            pl.BlockSpec((1, model_width, part), lambda l, s: (l, 0, s)),
            pl.BlockSpec((1, model_width, part), lambda l, s: (l, 0, s)),
        ],
        out_specs=pl.BlockSpec((count, part), lambda l, s: (0, l * 2 + s)),
        out_shape=jax.ShapeDtypeStruct((count, local_experts * width), jnp.bfloat16),
        compiler_params=pltpu.CompilerParams(vmem_limit_bytes=60 * MIB),
        name="stream_gate_up",
    )(inner_index, rows, w_gate, w_up)
    return pl.pallas_call(
        stream_down_kernel,
        grid=(model_width // TILE,),
        in_specs=[
            pl.BlockSpec(hidden.shape, lambda n: (0, 0)),
            pl.BlockSpec((local_experts, width, TILE), lambda n: (0, 0, n)),
        ],
        out_specs=pl.BlockSpec((count, TILE), lambda n: (0, n)),
        out_shape=jax.ShapeDtypeStruct((count, model_width), jnp.bfloat16),
        compiler_params=pltpu.CompilerParams(vmem_limit_bytes=60 * MIB),
        name="stream_down",
    )(hidden, w_down)


def load_kernel(source_ref, copy_ref, sem):
    copy = pltpu.make_async_copy(source_ref, copy_ref, sem)
    copy.start()
    copy.wait()


def load(weights):
    size = weights.size * weights.dtype.itemsize
    return pl.pallas_call(
        load_kernel,
        in_specs=[pl.BlockSpec(memory_space=pltpu.HBM)],
        out_specs=VMEM,
        out_shape=pltpu.VMEM(weights.shape, weights.dtype),
        scratch_shapes=[pltpu.SemaphoreType.DMA],
        compiler_params=pltpu.CompilerParams(vmem_limit_bytes=MIB),
        cost_estimate=pl.CostEstimate(flops=0, bytes_accessed=2 * size, transcendentals=0),
        name="load",
    )(weights)


def assemble(row_refs, x_ref):
    rows = jnp.concatenate([ref[...].astype(jnp.float32) for ref in row_refs])
    width = x_ref.shape[1]
    x_ref[...] = rows[:, :width].astype(jnp.bfloat16)
    return rows[:, width:]


def near_kernel(experts, blocks, index_ref, *refs):
    rows, (gate_w, up_source, out, up_w, x, gates, sems) = refs[:blocks], refs[blocks:]
    local_experts, _, width = gate_w.shape
    copies = [
        pltpu.make_async_copy(up_source.at[l], up_w.at[l], sems.at[l])
        for l in range(local_experts)
    ]
    for copy in copies:
        copy.start()
    columns = assemble(rows, x)
    ahead = local_experts // 2

    def gate_of(l):
        gates[:, l * width : (l + 1) * width] = jnp.dot(
            x[...], gate_w[l], preferred_element_type=jnp.float32
        )

    for l in range(ahead):
        gate_of(l)
    for l in range(local_experts):
        if l + ahead < local_experts:
            gate_of(l + ahead)
        part = slice(l * width, (l + 1) * width)
        weight = weight_of(columns, index_ref[0] * local_experts + l, experts)
        copies[l].wait()
        gate = gates[:, part]
        upper = jnp.dot(x[...], up_w[l], preferred_element_type=jnp.float32)
        out[:, part] = (gate / (1.0 + jnp.exp(-gate)) * upper * weight).astype(jnp.bfloat16)


def near_rows(blocks, w_gate, w_up, inner_index, experts):
    local_experts, model_width, width = w_gate.shape
    count = sum(block.shape[0] for block in blocks)
    return pl.pallas_call(
        functools.partial(near_kernel, experts, len(blocks)),
        in_specs=[SMEM] + [VMEM] * (len(blocks) + 1) + [HBM],
        out_specs=[VMEM] * 2,
        out_shape=[
            jax.ShapeDtypeStruct((count, local_experts * width), jnp.bfloat16),
            pltpu.VMEM(w_up.shape, w_up.dtype),
        ],
        scratch_shapes=[
            pltpu.VMEM((count, model_width), jnp.bfloat16),
            pltpu.VMEM((count, local_experts * width), jnp.float32),
            pltpu.SemaphoreType.DMA((local_experts,)),
        ],
        compiler_params=pltpu.CompilerParams(vmem_limit_bytes=8 * MIB),
        cost_estimate=pl.CostEstimate(
            flops=4 * count * model_width * width * local_experts,
            bytes_accessed=0,
            transcendentals=0,
        ),
        name="near_rows",
    )(inner_index, *blocks, w_gate, w_up)


def tile_copies(source_ref, slots_ref, sems):
    copies = []
    for at in range(0, source_ref.shape[2], TILE):
        slot = at // TILE % slots_ref.shape[0]
        copy = pltpu.make_async_copy(
            source_ref.at[:, :, pl.ds(at, TILE)], slots_ref.at[slot], sems.at[slot]
        )
        copies.append((at, slot, copy))
    return copies


def far_kernel(experts, blocks, cut, index_ref, *refs):
    rows, rest = refs[:blocks], refs[blocks:]
    gate_w, up_w, near, down_w, own, other, high_a, high_b = rest[:8]
    x, hidden, slots, sems = rest[8:]
    local_experts, _, width = gate_w.shape
    copies = tile_copies(down_w, slots, sems)
    for _, _, copy in copies[:SLOTS]:
        copy.start()
    columns = assemble(rows, x)
    count = near.shape[0]
    half = count // 2
    hidden[:count] = near[...]
    for l in range(local_experts):
        weight = weight_of(columns, index_ref[0] * local_experts + l, experts)
        hidden[count:, l * width : (l + 1) * width] = hidden_of(
            x[...], gate_w[l], up_w[l], weight
        )
    for i, (at, slot, copy) in enumerate(copies):
        copy.wait()
        value = jnp.dot(
            hidden[...],
            slots[slot].reshape(-1, TILE),
            preferred_element_type=jnp.float32,
        ).astype(jnp.bfloat16)
        if i + SLOTS < len(copies):
            copies[i + SLOTS][2].start()
        to = slice(at, at + TILE)
        own[:half, to] = value[:half]
        own[half:, to] = value[count : count + half]
        other[:half, to] = value[half:count]
        value = value[count + half :]
        other[half:, to] = value[: half // 2]
        if at < cut:
            high_a[:, to] = value[half // 2 :]
        else:
            high_b[:, at - cut : at - cut + TILE] = value[half // 2 :]


def far_rows(blocks, w_gate, w_up, near, w_down, inner_index, experts, cut):
    count, depth = near.shape
    local_experts, width, model_width = w_down.shape
    return pl.pallas_call(
        functools.partial(far_kernel, experts, len(blocks), cut),
        in_specs=[SMEM] + [VMEM] * (len(blocks) + 3) + [HBM],
        out_specs=[VMEM] * 4,
        out_shape=[
            jax.ShapeDtypeStruct(shape, jnp.bfloat16)
            for shape in (
                (count, model_width),
                (count * 3 // 4, model_width),
                (count // 4, cut),
                (count // 4, model_width - cut),
            )
        ],
        scratch_shapes=[
            pltpu.VMEM((count, model_width), jnp.bfloat16),
            pltpu.VMEM((2 * count, depth), jnp.bfloat16),
            pltpu.VMEM((SLOTS, local_experts, width, TILE), w_down.dtype),
            pltpu.SemaphoreType.DMA((SLOTS,)),
        ],
        compiler_params=pltpu.CompilerParams(vmem_limit_bytes=14 * MIB),
        name="far_rows",
    )(inner_index, *blocks, w_gate, w_up, near, w_down)


def swap_core(value):
    return lax.ppermute(value, "outer", [(0, 1), (1, 0)])


def swap_inner(value, bit):
    return lax.ppermute(value, "inner", [(i, i ^ bit) for i in range(8)])


def tie(*values):
    return lax.optimization_barrier(values)


def wide(value):
    return value.astype(jnp.float32)


def on_device(hidden_states, expert_ids, gate_scores, w_gate, w_up, w_down):
    local_experts, model_width, _ = w_gate.shape
    inner_size = lax.axis_size("inner")
    experts = local_experts * inner_size
    count = hidden_states.shape[0]
    inner_index = lax.axis_index("inner").astype(jnp.int32).reshape(1)
    own = with_routing(hidden_states, expert_ids, gate_scores, experts)
    if inner_size != 8 or lax.axis_size("outer") != 2:
        everyone = lax.all_gather(own, ("outer", "inner"), axis=0, tiled=True)
        outs = stream_rows(everyone, w_gate, w_up, w_down, inner_index, experts)
        return lax.psum_scatter(outs, ("outer", "inner"), scatter_dimension=0, tiled=True)

    w_gate, w_up, w_down = (
        pltpu.with_memory_space_constraint(w, pltpu.HBM) for w in (w_gate, w_up, w_down)
    )
    own, inner_index = tie(own, inner_index)
    z1, y0, z2 = swap_inner(own, 2), swap_inner(own, 1), swap_inner(own, 4)
    w_gate = load(w_gate)
    own, z1, z2, y0, w_gate = tie(own, z1, z2, y0, w_gate)
    z3, y1, y2 = swap_inner(own, 6), swap_inner(z1, 1), swap_inner(z2, 1)
    y3 = swap_inner(z3, 1)
    near = [own, z1, z2, z3]
    near += [swap_core(block) for block in near]
    hidden, w_up = near_rows(near, w_gate, w_up, inner_index, experts)
    hidden, y2, y3 = tie(hidden, y2, y3)
    far = [y0, y1, y2, y3]
    far += [swap_core(block) for block in far]

    cut = (model_width // LANES * 6 // 7) * LANES
    own, other, high_a, high_b = far_rows(
        far, w_gate, w_up, hidden, w_down, inner_index, experts, cut
    )
    half = 4 * count
    middle = half + 2 * count
    high_a = (wide(own[middle:, :cut]) + wide(swap_core(high_a))).astype(jnp.bfloat16)
    high_a, other = tie(high_a, other)
    across = swap_inner(high_a, 1)
    other = wide(own[:middle]) + wide(swap_core(other))
    near, low = other[:half].reshape(4, count, model_width), other[half:]

    def together(near_rows, far_rows):
        return jnp.concatenate([near_rows, far_rows]).astype(jnp.bfloat16)

    first, high_b = tie(together(near[1], low[count:]), high_b)
    one = swap_inner(first, 2)
    high_b = wide(own[middle:, cut:]) + wide(swap_core(high_b))
    high_b = high_b.reshape(2, count, -1)
    two, three = (
        swap_inner(together(near[2 + i][:, cut:], high_b[i]), 4 + 2 * i) for i in (0, 1)
    )
    sent = [
        swap_inner(
            (near[2 + i][:, :cut] + wide(across[i * count : (i + 1) * count])).astype(
                jnp.bfloat16
            ),
            4 + 2 * i,
        )
        for i in (0, 1)
    ]
    rest = wide(two) + wide(three)
    back = low[:count] + wide(one[count:])
    back = jnp.concatenate([back[:, :cut], back[:, cut:] + rest[count:]], axis=1)
    back = swap_inner(back.astype(jnp.bfloat16), 1)
    total = near[0] + wide(one[:count]) + wide(back)
    along = jnp.concatenate([wide(sent[0]) + wide(sent[1]), rest[:count]], axis=1)
    return (total + along).astype(jnp.bfloat16)


def solution(mesh):
    return jax.shard_map(
        on_device,
        mesh=mesh,
        in_specs=(
            P(("groups", "outer", "inner"), None),
            P(("groups", "outer", "inner"), None),
            P(("groups", "outer", "inner"), None),
            P("inner", None, "outer"),
            P("inner", None, "outer"),
            P("inner", "outer", None),
        ),
        out_specs=P(("groups", "outer", "inner"), None),
        check_vma=False,
    )
```

```python
import functools

import jax
import jax.numpy as jnp
from jax import lax
from jax.experimental import pallas as pl
from jax.experimental.pallas import tpu as pltpu
from jax.sharding import PartitionSpec as P

LANES = 128
MIB = 1024 * 1024
TILE = 512
SLOTS = 4
VMEM = pl.BlockSpec(memory_space=pltpu.VMEM)
HBM = pl.BlockSpec(memory_space=pltpu.HBM)
SMEM = pl.BlockSpec(memory_space=pltpu.SMEM)


def send_kernel(experts, rows_hbm, ids_hbm, scores_hbm, out_ref, rows, ids, scores, sems):
    pairs = ((rows_hbm, rows), (ids_hbm, ids), (scores_hbm, scores))
    copies = [pltpu.make_async_copy(*pair, sems.at[i]) for i, pair in enumerate(pairs)]
    for copy in copies:
        copy.start()
    copies[1].wait()
    copies[2].wait()
    sigmoid_vals = jax.nn.sigmoid(scores[...])
    weights = 2.5 * sigmoid_vals / jnp.sum(sigmoid_vals, axis=0, keepdims=True)
    top, count = weights.shape
    expert = lax.broadcasted_iota(jnp.int32, (experts, count), 0)
    dense = jnp.zeros((experts, count), jnp.float32)
    for k in range(top):
        dense += jnp.where(expert == ids[k : k + 1, :], weights[k : k + 1, :], 0.0)
    high = lax.reduce_precision(dense, 8, 7)
    rest = jnp.zeros((LANES - 2 * experts, count), jnp.float32)
    table = jnp.concatenate([high, dense - high, rest]).astype(jnp.bfloat16)
    same = lax.broadcasted_iota(jnp.int32, (count, count), 0)
    same = same == lax.broadcasted_iota(jnp.int32, (count, count), 1)
    columns = lax.dot_general(
        same.astype(jnp.float32).astype(jnp.bfloat16),
        table,
        (((1,), (1,)), ((), ())),
        preferred_element_type=jnp.float32,
    )
    width = rows.shape[1]
    out_ref[:, width:] = columns.astype(jnp.bfloat16)
    copies[0].wait()
    out_ref[:, :width] = rows[...]


def with_routing(rows, expert_ids, gate_scores, experts):
    count, width = rows.shape
    arrays = [
        pltpu.with_memory_space_constraint(array, pltpu.HBM)
        for array in (rows, expert_ids.T, gate_scores.T)
    ]
    return pl.pallas_call(
        functools.partial(send_kernel, experts),
        in_specs=[HBM] * 3,
        out_specs=VMEM,
        out_shape=jax.ShapeDtypeStruct((count, width + LANES), jnp.bfloat16),
        scratch_shapes=[pltpu.VMEM(array.shape, array.dtype) for array in arrays]
        + [pltpu.SemaphoreType.DMA((3,))],
        compiler_params=pltpu.CompilerParams(vmem_limit_bytes=4 * MIB),
        name="with_routing",
    )(*arrays)


def weight_of(columns, expert, experts):
    lane = lax.broadcasted_iota(jnp.int32, columns.shape, 1)
    mine = (lane == expert) | (lane == expert + experts)
    return jnp.sum(jnp.where(mine, columns, 0.0), axis=1, keepdims=True)


def hidden_of(x, gate_w, up_w, weight):
    gate = jnp.dot(x, gate_w, preferred_element_type=jnp.float32)
    upper = jnp.dot(x, up_w, preferred_element_type=jnp.float32)
    return (gate / (1.0 + jnp.exp(-gate)) * upper * weight).astype(jnp.bfloat16)


def stream_up_kernel(experts, local_experts, index_ref, rows_ref, gate_w_ref, up_w_ref, out_ref):
    model_width = gate_w_ref.shape[1]
    expert = index_ref[0] * local_experts + pl.program_id(0)
    weight = weight_of(rows_ref[:, model_width:].astype(jnp.float32), expert, experts)
    out_ref[...] = hidden_of(rows_ref[:, :model_width], gate_w_ref[0], up_w_ref[0], weight)


def stream_down_kernel(hidden_ref, down_w_ref, out_ref):
    block = down_w_ref[...]
    block = block.reshape(block.shape[0] * block.shape[1], block.shape[2])
    out_ref[...] = jnp.dot(
        hidden_ref[...], block, preferred_element_type=jnp.float32
    ).astype(jnp.bfloat16)


def stream_rows(rows, w_gate, w_up, w_down, inner_index, experts):
    local_experts, model_width, width = w_gate.shape
    count, part = rows.shape[0], width // 2
    hidden = pl.pallas_call(
        functools.partial(stream_up_kernel, experts, local_experts),
        grid=(local_experts, 2),
        in_specs=[
            pl.BlockSpec(memory_space=pltpu.SMEM),
            pl.BlockSpec((count, rows.shape[1]), lambda l, s: (0, 0)),
            pl.BlockSpec((1, model_width, part), lambda l, s: (l, 0, s)),
            pl.BlockSpec((1, model_width, part), lambda l, s: (l, 0, s)),
        ],
        out_specs=pl.BlockSpec((count, part), lambda l, s: (0, l * 2 + s)),
        out_shape=jax.ShapeDtypeStruct((count, local_experts * width), jnp.bfloat16),
        compiler_params=pltpu.CompilerParams(vmem_limit_bytes=60 * MIB),
        name="stream_gate_up",
    )(inner_index, rows, w_gate, w_up)
    return pl.pallas_call(
        stream_down_kernel,
        grid=(model_width // TILE,),
        in_specs=[
            pl.BlockSpec(hidden.shape, lambda n: (0, 0)),
            pl.BlockSpec((local_experts, width, TILE), lambda n: (0, 0, n)),
        ],
        out_specs=pl.BlockSpec((count, TILE), lambda n: (0, n)),
        out_shape=jax.ShapeDtypeStruct((count, model_width), jnp.bfloat16),
        compiler_params=pltpu.CompilerParams(vmem_limit_bytes=60 * MIB),
        name="stream_down",
    )(hidden, w_down)


def load_kernel(source_ref, copy_ref, sem):
    copy = pltpu.make_async_copy(source_ref, copy_ref, sem)
    copy.start()
    copy.wait()


def load(weights):
    size = weights.size * weights.dtype.itemsize
    return pl.pallas_call(
        load_kernel,
        in_specs=[pl.BlockSpec(memory_space=pltpu.HBM)],
        out_specs=VMEM,
        out_shape=pltpu.VMEM(weights.shape, weights.dtype),
        scratch_shapes=[pltpu.SemaphoreType.DMA],
        compiler_params=pltpu.CompilerParams(vmem_limit_bytes=MIB),
        cost_estimate=pl.CostEstimate(flops=0, bytes_accessed=2 * size, transcendentals=0),
        name="load",
    )(weights)


def assemble(row_refs, x_ref):
    rows = jnp.concatenate([ref[...].astype(jnp.float32) for ref in row_refs])
    width = x_ref.shape[1]
    x_ref[...] = rows[:, :width].astype(jnp.bfloat16)
    return rows[:, width:]


def near_kernel(experts, blocks, index_ref, *refs):
    rows, (gate_w, up_source, out, up_w, x, gates, sems) = refs[:blocks], refs[blocks:]
    local_experts, _, width = gate_w.shape
    copies = [
        pltpu.make_async_copy(up_source.at[l], up_w.at[l], sems.at[l])
        for l in range(local_experts)
    ]
    for copy in copies:
        copy.start()
    columns = assemble(rows, x)
    ahead = local_experts // 2

    def gate_of(l):
        gates[:, l * width : (l + 1) * width] = jnp.dot(
            x[...], gate_w[l], preferred_element_type=jnp.float32
        )

    for l in range(ahead):
        gate_of(l)
    for l in range(local_experts):
        if l + ahead < local_experts:
            gate_of(l + ahead)
        part = slice(l * width, (l + 1) * width)
        weight = weight_of(columns, index_ref[0] * local_experts + l, experts)
        copies[l].wait()
        gate = gates[:, part]
        upper = jnp.dot(x[...], up_w[l], preferred_element_type=jnp.float32)
        out[:, part] = (gate / (1.0 + jnp.exp(-gate)) * upper * weight).astype(jnp.bfloat16)


def near_rows(blocks, w_gate, w_up, inner_index, experts):
    local_experts, model_width, width = w_gate.shape
    count = sum(block.shape[0] for block in blocks)
    return pl.pallas_call(
        functools.partial(near_kernel, experts, len(blocks)),
        in_specs=[SMEM] + [VMEM] * (len(blocks) + 1) + [HBM],
        out_specs=[VMEM] * 2,
        out_shape=[
            jax.ShapeDtypeStruct((count, local_experts * width), jnp.bfloat16),
            pltpu.VMEM(w_up.shape, w_up.dtype),
        ],
        scratch_shapes=[
            pltpu.VMEM((count, model_width), jnp.bfloat16),
            pltpu.VMEM((count, local_experts * width), jnp.float32),
            pltpu.SemaphoreType.DMA((local_experts,)),
        ],
        compiler_params=pltpu.CompilerParams(vmem_limit_bytes=8 * MIB),
        cost_estimate=pl.CostEstimate(
            flops=4 * count * model_width * width * local_experts,
            bytes_accessed=0,
            transcendentals=0,
        ),
        name="near_rows",
    )(inner_index, *blocks, w_gate, w_up)


def tile_copies(source_ref, slots_ref, sems):
    copies = []
    for at in range(0, source_ref.shape[2], TILE):
        slot = at // TILE % slots_ref.shape[0]
        copy = pltpu.make_async_copy(
            source_ref.at[:, :, pl.ds(at, TILE)], slots_ref.at[slot], sems.at[slot]
        )
        copies.append((at, slot, copy))
    return copies


def far_kernel(experts, blocks, cut, index_ref, *refs):
    rows, rest = refs[:blocks], refs[blocks:]
    gate_w, up_w, near, down_w, own, other, high_a, high_b = rest[:8]
    x, hidden, slots, sems = rest[8:]
    local_experts, _, width = gate_w.shape
    copies = tile_copies(down_w, slots, sems)
    for _, _, copy in copies[:SLOTS]:
        copy.start()
    columns = assemble(rows, x)
    count = near.shape[0]
    half = count // 2
    hidden[:count] = near[...]
    for l in range(local_experts):
        weight = weight_of(columns, index_ref[0] * local_experts + l, experts)
        hidden[count:, l * width : (l + 1) * width] = hidden_of(
            x[...], gate_w[l], up_w[l], weight
        )
    for i, (at, slot, copy) in enumerate(copies):
        copy.wait()
        value = jnp.dot(
            hidden[...],
            slots[slot].reshape(-1, TILE),
            preferred_element_type=jnp.float32,
        ).astype(jnp.bfloat16)
        if i + SLOTS < len(copies):
            copies[i + SLOTS][2].start()
        to = slice(at, at + TILE)
        own[:half, to] = value[:half]
        own[half:, to] = value[count : count + half]
        other[:half, to] = value[half:count]
        value = value[count + half :]
        other[half:, to] = value[: half // 2]
        if at < cut:
            high_a[:, to] = value[half // 2 :]
        else:
            high_b[:, at - cut : at - cut + TILE] = value[half // 2 :]


def far_rows(blocks, w_gate, w_up, near, w_down, inner_index, experts, cut):
    count, depth = near.shape
    local_experts, width, model_width = w_down.shape
    return pl.pallas_call(
        functools.partial(far_kernel, experts, len(blocks), cut),
        in_specs=[SMEM] + [VMEM] * (len(blocks) + 3) + [HBM],
        out_specs=[VMEM] * 4,
        out_shape=[
            jax.ShapeDtypeStruct(shape, jnp.bfloat16)
            for shape in (
                (count, model_width),
                (count * 3 // 4, model_width),
                (count // 4, cut),
                (count // 4, model_width - cut),
            )
        ],
        scratch_shapes=[
            pltpu.VMEM((count, model_width), jnp.bfloat16),
            pltpu.VMEM((2 * count, depth), jnp.bfloat16),
            pltpu.VMEM((SLOTS, local_experts, width, TILE), w_down.dtype),
            pltpu.SemaphoreType.DMA((SLOTS,)),
        ],
        compiler_params=pltpu.CompilerParams(vmem_limit_bytes=14 * MIB),
        name="far_rows",
    )(inner_index, *blocks, w_gate, w_up, near, w_down)


def swap_core(value):
    return lax.ppermute(value, "outer", [(0, 1), (1, 0)])


def swap_inner(value, bit):
    return lax.ppermute(value, "inner", [(i, i ^ bit) for i in range(8)])


def tie(*values):
    return lax.optimization_barrier(values)


def wide(value):
    return value.astype(jnp.float32)


def on_device(hidden_states, expert_ids, gate_scores, w_gate, w_up, w_down):
    local_experts, model_width, _ = w_gate.shape
    inner_size = lax.axis_size("inner")
    experts = local_experts * inner_size
    count = hidden_states.shape[0]
    inner_index = lax.axis_index("inner").astype(jnp.int32).reshape(1)
    own = with_routing(hidden_states, expert_ids, gate_scores, experts)
    if inner_size != 8 or lax.axis_size("outer") != 2:
        everyone = lax.all_gather(own, ("outer", "inner"), axis=0, tiled=True)
        outs = stream_rows(everyone, w_gate, w_up, w_down, inner_index, experts)
        return lax.psum_scatter(outs, ("outer", "inner"), scatter_dimension=0, tiled=True)

    w_gate, w_up, w_down = (
        pltpu.with_memory_space_constraint(w, pltpu.HBM) for w in (w_gate, w_up, w_down)
    )
    own, inner_index = tie(own, inner_index)
    z1, y0, z2 = swap_inner(own, 2), swap_inner(own, 1), swap_inner(own, 4)
    again, z1, y0, source = tie(own, z1, y0, w_gate)
    z3, y1 = swap_inner(again, 6), swap_inner(z1, 1)
    w_gate = load(source)
    z2, w_gate = tie(z2, w_gate)
    y2, y3 = swap_inner(z2, 1), swap_inner(z3, 1)
    near = [own, z1, z2, z3]
    near += [swap_core(block) for block in near]
    hidden, w_up = near_rows(near, w_gate, w_up, inner_index, experts)
    hidden, y2, y3 = tie(hidden, y2, y3)
    far = [y0, y1, y2, y3]
    far += [swap_core(block) for block in far]

    cut = (model_width // LANES * 6 // 7) * LANES
    own, other, high_a, high_b = far_rows(
        far, w_gate, w_up, hidden, w_down, inner_index, experts, cut
    )
    half = 4 * count
    middle = half + 2 * count
    high_a = (wide(own[middle:, :cut]) + wide(swap_core(high_a))).astype(jnp.bfloat16)
    across = swap_inner(high_a, 1)
    other = wide(own[:middle]) + wide(swap_core(other))
    high_b = wide(own[middle:, cut:]) + wide(swap_core(high_b))
    near, low = other[:half].reshape(4, count, model_width), other[half:]
    high_b = high_b.reshape(2, count, -1)

    def together(near_rows, far_rows):
        return jnp.concatenate([near_rows, far_rows]).astype(jnp.bfloat16)

    one = swap_inner(together(near[1], low[count:]), 2)
    two, three = (
        swap_inner(together(near[2 + i][:, cut:], high_b[i]), 4 + 2 * i) for i in (0, 1)
    )
    sent = [
        swap_inner(
            (near[2 + i][:, :cut] + wide(across[i * count : (i + 1) * count])).astype(
                jnp.bfloat16
            ),
            4 + 2 * i,
        )
        for i in (0, 1)
    ]
    rest = wide(two) + wide(three)
    back = low[:count] + wide(one[count:])
    back = jnp.concatenate([back[:, :cut], back[:, cut:] + rest[count:]], axis=1)
    back = swap_inner(back.astype(jnp.bfloat16), 1)
    total = near[0] + wide(one[:count]) + wide(back)
    along = jnp.concatenate([wide(sent[0]) + wide(sent[1]), rest[:count]], axis=1)
    return (total + along).astype(jnp.bfloat16)


def solution(mesh):
    return jax.shard_map(
        on_device,
        mesh=mesh,
        in_specs=(
            P(("groups", "outer", "inner"), None),
            P(("groups", "outer", "inner"), None),
            P(("groups", "outer", "inner"), None),
            P("inner", None, "outer"),
            P("inner", None, "outer"),
            P("inner", "outer", None),
        ),
        out_specs=P(("groups", "outer", "inner"), None),
        check_vma=False,
    )
```
